32 devices in a mesh: groups: 2 (over y), store: 4 (over x, core), tensor: 4 (over z).
Axes of the slice: x: 2, y: 2, z: 4, core: 2. Of those that a mesh axis runs over, the one named last changes fastest.
Arguments:
- tokens: bfloat16 [112, 8192], P(('groups', 'tensor'), 'store'), parts along dimension 0, may hold values from -6 to 6
- adapter_ids: int32 [112], P('groups'), parts along dimension 0, may hold values from 0 to 31
- store_slot: int32 [32], replicated, may hold values from 0 to 31, each once
- w_gate: bfloat16 [8192, 14336], P('store', 'tensor'), may hold values from -0.0625 to 0.0625
- w_up: bfloat16 [8192, 14336], P('store', 'tensor'), may hold values from -0.0625 to 0.0625
- w_down: bfloat16 [14336, 8192], P('tensor', 'store'), may hold values from -0.046875 to 0.046875
- a_gate: bfloat16 [32, 16, 8192], P('tensor', None, 'store'), may hold values from -0.0625 to 0.0625
- b_gate: bfloat16 [32, 16, 14336], P('store', None, 'tensor'), may hold values from -1.5 to 1.5
- a_up: bfloat16 [32, 16, 8192], P('tensor', None, 'store'), may hold values from -0.0625 to 0.0625
- b_up: bfloat16 [32, 16, 14336], P('store', None, 'tensor'), may hold values from -1.5 to 1.5
- a_down: bfloat16 [32, 16, 14336], P('store', None, 'tensor'), may hold values from -0.046875 to 0.046875
- b_down: bfloat16 [32, 16, 8192], P('tensor', None, 'store'), may hold values from -1.5 to 1.5
Outputs:
- mixed: bfloat16 [112, 8192], P(('groups', 'tensor'), 'store'), parts along dimension 0
The draws below stay inside these ranges and needn't reach their ends.
There are 2 independent parts, one for each index of `groups`. The reference program is written for one: setup_inputs(seed, part) draws one part's arguments, and reference() takes and returns one part's arrays. A program takes and returns all parts, laid end to end along the dimension named above; an argument that names none is the same for every part. Nothing has to cross between parts.
Inputs may be any that keep to these rules, and one draw needn't show every extreme that they name: `adapter_ids`: adapter of each request, an index into store_slot. `store_slot`: every store place is used by exactly one adapter.
All inputs are finite; a program needn't handle non-finite values.
Results may differ from the reference program's by a relative error of at most 0.0062.
Values may be sent and summed in bfloat16 or wider, within the bound.
A program may use at most 128 MiB of HBM per device.

```python
import math
import jax
import jax.numpy as jnp
import numpy as np

D = 8192
FF = 14336
RANK = 16
TOKENS = 56
NADP = 32


def place_ends(array, stream_key, smallest, top_value):
    extent = array.shape
    spot = [jax.random.randint(jax.random.fold_in(stream_key, axis), (), 0, extent[axis]) for axis in range(len(extent))]
    array = array.at[tuple(spot)].set(smallest)
    longest = extent.index(max(extent))
    spot[longest] = (spot[longest] + 1) % extent[longest]
    return array.at[tuple(spot)].set(top_value)


def shard_levels(own_key, dims, shards, least, high):
    gain = 1.0
    for position, shards_of in shards:
        heights = jax.random.uniform(jax.random.fold_in(jax.random.fold_in(own_key, 6), position), (shards_of,), jnp.float32, least / len(shards), high / len(shards))
        gain = gain * jnp.repeat(jnp.exp(heights), dims[position] // shards_of).reshape((-1,) + (1,) * (len(dims) - 1 - position))
    return gain


def cumulative_ranks(amount, skew):
    weights = [(1 << 20) // math.isqrt(rank ** skew) + 1 for rank in range(1, amount + 1)]
    scale = 1 + sum(weights) // (1 << 30)
    return np.cumsum(np.array([max(1, weight // scale) for weight in weights]))


def ranked(stream_key, extent, number_of, skew):
    listing = cumulative_ranks(number_of, skew)
    ticket = jax.random.randint(jax.random.fold_in(stream_key, 1), extent, 0, int(listing[number_of - 1]))
    grade = jnp.searchsorted(jnp.asarray(listing, jnp.int32), ticket, side="right")
    return jax.random.permutation(jax.random.fold_in(stream_key, 2), number_of)[grade].astype(jnp.int32)


def bell_draw(rng, shape, scale, limit, cuts=(), held_as=jnp.bfloat16):
    result = jax.random.normal(rng, shape, jnp.float32) * scale
    if len(cuts) > 0:
        result = shard_levels(rng, shape, cuts, -0.22, 0.18) * result
    return jnp.clip(result, min=-limit, max=limit).astype(held_as)


def setup_inputs(seed: int = 0, part: int = 0) -> dict:
    keys = jax.random.split(jax.random.key(seed), 13)
    part_splits = jax.random.split(jax.random.fold_in(keys[12], part), 13)
    return {
        "tokens": bell_draw(part_splits[0], (TOKENS, D), 1.0, 6.0, ((0, 4), (1, 4))),
        "adapter_ids": place_ends(ranked(part_splits[1], (TOKENS,), NADP, 2), jax.random.fold_in(part_splits[1], 3), 0, NADP - 1).astype(jnp.int32),
        "store_slot": jax.random.permutation(keys[2], NADP).astype(jnp.int32),
        "w_gate": bell_draw(keys[3], (D, FF), D ** -0.5, 0.0625, ((0, 4), (1, 4))),
        "w_up": bell_draw(keys[4], (D, FF), D ** -0.5, 0.0625, ((0, 4), (1, 4))),
        "w_down": bell_draw(keys[5], (FF, D), FF ** -0.5, 0.046875, ((0, 4), (1, 4))),
        "a_gate": bell_draw(keys[6], (NADP, RANK, D), D ** -0.5, 0.0625, ((0, 4), (2, 4))),
        "b_gate": bell_draw(keys[7], (NADP, RANK, FF), RANK ** -0.5, 1.5, ((0, 4), (2, 4))),
        "a_up": bell_draw(keys[8], (NADP, RANK, D), D ** -0.5, 0.0625, ((0, 4), (2, 4))),
        "b_up": bell_draw(keys[9], (NADP, RANK, FF), RANK ** -0.5, 1.5, ((0, 4), (2, 4))),
        "a_down": bell_draw(keys[10], (NADP, RANK, FF), FF ** -0.5, 0.046875, ((0, 4), (2, 4))),
        "b_down": bell_draw(keys[11], (NADP, RANK, D), RANK ** -0.5, 1.5, ((0, 4), (2, 4))),
    }


def pick_rank(products, place_hot):
    shaped = products.reshape(products.shape[0], place_hot.shape[1], -1)
    return jnp.sum(shaped * place_hot[:, :, None], axis=1)


def spread_rank(low_rank, place_hot):
    spread = place_hot.astype(jnp.bfloat16)[:, :, None] * low_rank[:, None, :]
    return spread.reshape(low_rank.shape[0], -1)


def reference(tokens, adapter_ids, store_slot, w_gate, w_up, w_down, a_gate, b_gate, a_up, b_up, a_down, b_down):
    id_hot = adapter_ids[:, None] == jnp.arange(NADP, dtype=jnp.int32)[None, :]
    place = jnp.sum(jnp.where(id_hot, store_slot[None, :], 0), axis=1).astype(jnp.int32)
    place_hot = (place[:, None] == jnp.arange(NADP, dtype=jnp.int32)[None, :]).astype(jnp.float32)
    gate_low = pick_rank(jnp.dot(tokens, a_gate.reshape(-1, D).T, preferred_element_type=jnp.float32), place_hot).astype(jnp.bfloat16)
    up_low = pick_rank(jnp.dot(tokens, a_up.reshape(-1, D).T, preferred_element_type=jnp.float32), place_hot).astype(jnp.bfloat16)
    gate = jnp.dot(tokens, w_gate, preferred_element_type=jnp.float32) + jnp.dot(spread_rank(gate_low, place_hot), b_gate.reshape(-1, FF), preferred_element_type=jnp.float32)
    up = jnp.dot(tokens, w_up, preferred_element_type=jnp.float32) + jnp.dot(spread_rank(up_low, place_hot), b_up.reshape(-1, FF), preferred_element_type=jnp.float32)
    hidden = (jax.nn.silu(gate) * up).astype(jnp.bfloat16)
    down_low = pick_rank(jnp.dot(hidden, a_down.reshape(-1, FF).T, preferred_element_type=jnp.float32), place_hot).astype(jnp.bfloat16)
    mixed = jnp.dot(hidden, w_down, preferred_element_type=jnp.float32) + jnp.dot(spread_rank(down_low, place_hot), b_down.reshape(-1, D), preferred_element_type=jnp.float32)
    return mixed.astype(jnp.bfloat16)
```

```python
import functools

import jax
import jax.numpy as jnp
from jax import lax
from jax.experimental import pallas as pl
from jax.experimental.pallas import tpu as pltpu
from jax.sharding import PartitionSpec as P

MESH = pl.DeviceIdType.MESH
BF = jnp.bfloat16
F32 = jnp.float32
PAD = 16
CHUNKS = 7
OUT_CHUNKS = 4
LAG_B, LAG_H, LAG_F, LAG_D = 1, 2, 3, 4


def nt_dot(a, b):
    return lax.dot_general(a, b, (((1,), (1,)), ((), ())), preferred_element_type=F32)


def kernel(
    S,
    T,
    rank,
    tok_ref,
    ids_ref,
    slot_ref,
    wg_hbm,
    wu_hbm,
    wd_hbm,
    ag_hbm,
    bg_hbm,
    au_hbm,
    bu_hbm,
    ad_hbm,
    bd_hbm,
    out_ref,
    wg,
    wu,
    wd,
    ag,
    bg,
    au,
    bu,
    ad,
    bd,
    tok,
    hot_t,
    hot_s,
    acc,
    send_a,
    recv_a,
    send_b,
    recv_b,
    hid,
    lacc,
    oacc,
    osend,
    orecv,
    low_mine,
    low_store,
    low_sum,
    low_tensor,
    dlow_mine,
    dlow_store,
    dlow_sum,
    dlow_tensor,
    w_sem,
    f_sem,
    tok_ss,
    tok_rs,
    ls_ss,
    ls_rs,
    lt_ss,
    lt_rs,
    ds_ss,
    ds_rs,
    dt_ss,
    dt_rs,
    a_ss,
    a_rs,
    b_ss,
    b_rs,
    h_ss,
    h_rs,
    g_ss,
    g_rs,
    k_ss,
    k_rs,
    o_ss,
    o_rs,
):
    X = S // 2
    s = lax.axis_index("store")
    t = lax.axis_index("tensor")
    x, c = s // 2, s % 2
    sib = x * 2 + (1 - c)
    n = tok_ref.shape[0]
    rows = T * PAD
    depth = tok.shape[2]
    nc = wg.shape[2]
    lanes = ag.shape[0]
    groups = lanes // rank
    on = oacc.shape[2]

    def weight(hbm, buf, j, sem):
        return pltpu.make_async_copy(hbm.at[:, pl.ds(j * nc, nc)], buf.at[j], sem)

    cg = [weight(wg_hbm, wg, j, w_sem.at[0, j]) for j in range(CHUNKS)]
    cu = [weight(wu_hbm, wu, j, w_sem.at[1, j]) for j in range(CHUNKS)]
    cd = [
        pltpu.make_async_copy(wd_hbm.at[pl.ds(j * nc, nc), :], wd.at[j], w_sem.at[2, j])
        for j in range(CHUNKS)
    ]
    cag = pltpu.make_async_copy(ag_hbm, ag, f_sem.at[0])
    cau = pltpu.make_async_copy(au_hbm, au, f_sem.at[1])
    cbg = pltpu.make_async_copy(bg_hbm, bg, f_sem.at[2])
    cbu = pltpu.make_async_copy(bu_hbm, bu, f_sem.at[3])
    cad = pltpu.make_async_copy(ad_hbm, ad, f_sem.at[4])
    cbd = pltpu.make_async_copy(bd_hbm, bd, f_sem.at[5])

    barrier = pltpu.get_barrier_semaphore()
    for d in range(1, S):
        pl.semaphore_signal(
            barrier, inc=1, device_id={"store": (s + d) % S}, device_id_type=MESH
        )
    for d in range(1, T):
        pl.semaphore_signal(
            barrier, inc=1, device_id={"tensor": (t + d) % T}, device_id_type=MESH
        )
    cag.start()
    cau.start()
    for j in range(CHUNKS):
        cg[j].start()
        cu[j].start()
        if j == 1:
            cbg.start()
            cbu.start()
    cad.start()
    for j in range(CHUNKS):
        cd[j].start()
    cbd.start()

    tok[t] = jnp.zeros((PAD, depth), BF)
    tok[t, 0:n, :] = tok_ref[...]
    pl.semaphore_wait(barrier, S + T - 2)

    def remote(src, dst, ss, rs, axis, index):
        return pltpu.make_async_remote_copy(
            src_ref=src,
            dst_ref=dst,
            send_sem=ss,
            recv_sem=rs,
            device_id={axis: index},
            device_id_type=MESH,
        )

    sent = []

    def go(copy):
        copy.start()
        sent.append(copy)
        return copy

    tcopies = [
        go(remote(tok.at[t], tok.at[t], tok_ss.at[d - 1], tok_rs.at[d - 1], "tensor", (t + d) % T))
        for d in range(1, T)
    ]

    lane_group = lax.broadcasted_iota(jnp.int32, (1, lanes), 1) // rank
    hot_t[...] = jnp.zeros_like(hot_t)
    hot_s[...] = jnp.zeros_like(hot_s)

    def mark(r, carry):
        place = slot_ref[ids_ref[r]]
        row = (r // n) * PAD + r % n
        hot_t[pl.ds(row, 1), :] = jnp.where(lane_group == place - t * groups, 1.0, 0.0)
        hot_s[pl.ds(row, 1), :] = jnp.where(lane_group == place - s * groups, 1.0, 0.0)
        return carry

    lax.fori_loop(0, n * T, mark, 0)

    fold = (
        lax.broadcasted_iota(jnp.int32, (lanes, lanes), 0) % rank
        == lax.broadcasted_iota(jnp.int32, (lanes, lanes), 1) % rank
    )
    own_group = (
        lax.broadcasted_iota(jnp.int32, (rows, lanes), 0) % groups
        == lax.broadcasted_iota(jnp.int32, (rows, lanes), 1) // rank
    )

    def pack(part):
        spread = jnp.dot(
            part, fold.astype(F32), precision=lax.Precision.HIGHEST, preferred_element_type=F32
        )
        spread = jnp.where(own_group, spread, 0.0)
        return jnp.sum(spread.reshape(rows // groups, groups, lanes), axis=1)

    def unpack(packed, hot):
        spread = jnp.broadcast_to(packed[:, None, :], (rows // groups, groups, lanes))
        spread = jnp.where(own_group, spread.reshape(rows, lanes), 0.0).astype(BF)
        low = jnp.dot(spread, fold.astype(F32).astype(BF), preferred_element_type=F32)
        return (low * hot[...]).astype(BF)

    def exchange(mine, slots, ss, rs, axis, me, size):
        return [
            go(remote(mine, slots.at[d - 1], ss.at[d - 1], rs.at[d - 1], axis, (me + d) % size))
            for d in range(1, size)
        ]

    def gather_sum(mine, slots, copies):
        total = mine[...]
        for d, copy in enumerate(copies):
            copy.wait_recv()
            total = total + slots[d]
        return total

    for copy in tcopies:
        copy.wait_recv()
    tokens = tok[...].reshape(rows, depth)

    cag.wait()
    cau.wait()
    low_mine[0] = pack(nt_dot(tokens, ag[...]) * hot_t[...])
    low_mine[1] = pack(nt_dot(tokens, au[...]) * hot_t[...])
    ls = exchange(low_mine, low_store, ls_ss, ls_rs, "store", s, S)

    q = rows // S

    def main(j):
        cg[j].wait()
        g = jnp.dot(tok[...].reshape(rows, depth), wg[j], preferred_element_type=F32)
        acc[j, :, :, 0:nc] = g.reshape(S, q, nc)
        cu[j].wait()
        u = jnp.dot(tok[...].reshape(rows, depth), wu[j], preferred_element_type=F32)
        acc[j, :, :, nc:] = u.reshape(S, q, nc)

    acopies, bcopies, hcopies, gcopies, kcopies = {}, {}, {}, {}, {}

    def finish(j, spread_g, spread_u):
        cols = pl.ds(j * nc, nc)
        acc[j, :, :, 0:nc] += jnp.dot(
            spread_g, bg[:, cols], preferred_element_type=F32
        ).reshape(S, q, nc)
        acc[j, :, :, nc:] += jnp.dot(
            spread_u, bu[:, cols], preferred_element_type=F32
        ).reshape(S, q, nc)
        for k in range(X):
            send_a[j, k] = acc[j, 2 * k + (1 - c)].astype(BF)
        acopies[j] = go(remote(send_a.at[j], recv_a.at[j], a_ss.at[j], a_rs.at[j], "store", sib))

    def stage_b(j):
        acopies[j].wait_recv()
        bcopies[j] = []
        for d in range(1, X):
            xo = (x + d) % X
            send_b[j, d - 1] = (acc[j, 2 * xo + c] + recv_a[j, xo].astype(F32)).astype(BF)
            bcopies[j].append(
                go(
                    remote(
                        send_b.at[j, d - 1],
                        recv_b.at[j, d - 1],
                        b_ss.at[j, d - 1],
                        b_rs.at[j, d - 1],
                        "store",
                        xo * 2 + c,
                    )
                )
            )

    def stage_h(j):
        total = acc[j, s] + recv_a[j, x].astype(F32)
        for d in range(1, X):
            bcopies[j][d - 1].wait_recv()
            total = total + recv_b[j, d - 1].astype(F32)
        gate, up = total[:, 0:nc], total[:, nc:]
        hid[j, s] = (gate / (1.0 + jnp.exp(-gate)) * up).astype(BF)
        gcopies[j] = [
            go(
                remote(
                    hid.at[j, s],
                    hid.at[j, s],
                    g_ss.at[j, d - 1],
                    g_rs.at[j, d - 1],
                    "store",
                    ((x + d) % X) * 2 + c,
                )
            )
            for d in range(1, X)
        ]
        hcopies[j] = go(
            remote(hid.at[j, s], hid.at[j, s], h_ss.at[j], h_rs.at[j], "store", sib)
        )

    def stage_f(j):
        kcopies[j] = []
        for d in range(1, X):
            gcopies[j][d - 1].wait_recv()
            origin = ((x - d + X) % X) * 2 + c
            kcopies[j].append(
                go(
                    remote(
                        hid.at[j, origin],
                        hid.at[j, origin],
                        k_ss.at[j, d - 1],
                        k_rs.at[j, d - 1],
                        "store",
                        sib,
                    )
                )
            )

    def stage_d(j):
        hcopies[j].wait_recv()
        for copy in kcopies[j]:
            copy.wait_recv()
        h = hid[j].reshape(rows, nc)
        if j == 0:
            cad.wait()
        low = nt_dot(h, ad[:, pl.ds(j * nc, nc)])
        lacc[...] = low if j == 0 else lacc[...] + low
        last = j == CHUNKS - 1
        copies = None
        if last:
            dlow_mine[...] = pack(lacc[...] * hot_s[...])
            copies = exchange(dlow_mine, dlow_store, ds_ss, ds_rs, "store", s, S)
        cd[j].wait()
        half = OUT_CHUNKS // 2
        for k in range(OUT_CHUNKS):
            if last and k == half:
                dlow_sum[...] = gather_sum(dlow_mine, dlow_store, copies)
                copies = exchange(dlow_sum, dlow_tensor, dt_ss, dt_rs, "tensor", t, T)
            o = jnp.dot(
                hid[j].reshape(rows, nc), wd[j, :, k * on : (k + 1) * on], preferred_element_type=F32
            )
            oacc[k] = o if j == 0 else oacc[k] + o
        return copies

    main(0)
    low_sum[...] = gather_sum(low_mine, low_store, ls)
    lt = exchange(low_sum, low_tensor, lt_ss, lt_rs, "tensor", t, T)
    main(1)
    main(2)
    low = gather_sum(low_sum, low_tensor, lt)
    spread_g = unpack(low[0], hot_s)
    spread_u = unpack(low[1], hot_s)
    cbg.wait()
    cbu.wait()

    copies = None
    done_h = 0
    for i in range(CHUNKS + LAG_D):
        if 3 <= i < CHUNKS:
            main(i)
        if i < CHUNKS:
            finish(i, spread_g, spread_u)
        if 0 <= i - LAG_B < CHUNKS:
            stage_b(i - LAG_B)
        if 0 <= i - LAG_H < CHUNKS:
            stage_h(i - LAG_H)
        if 0 <= i - LAG_F < CHUNKS:
            stage_f(i - LAG_F)
        if 0 <= i - LAG_D < CHUNKS:
            copies = stage_d(i - LAG_D)

    dlow = gather_sum(dlow_sum, dlow_tensor, copies)
    spread_d = unpack(dlow, hot_t)
    cbd.wait()
    ocopies = []
    own = []
    for k in range(OUT_CHUNKS):
        o = oacc[k] + jnp.dot(
            spread_d, bd[:, k * on : (k + 1) * on], preferred_element_type=F32
        )
        oacc[k] = o
        osend[k] = o.reshape(T, PAD, on).astype(BF)
        ocopies.append(
            [
                go(
                    remote(
                        osend.at[k, (t + d) % T],
                        orecv.at[k, d - 1],
                        o_ss.at[k, d - 1],
                        o_rs.at[k, d - 1],
                        "tensor",
                        (t + d) % T,
                    )
                )
                for d in range(1, T)
            ]
        )
    for k in range(OUT_CHUNKS):
        total = oacc[k, pl.ds(pl.multiple_of(t * PAD, PAD), PAD), :]
        for d in range(1, T):
            ocopies[k][d - 1].wait_recv()
            total = total + orecv[k, d - 1].astype(F32)
        out_ref[:, k * on : (k + 1) * on] = total[0:n].astype(BF)
    for copy in sent:
        copy.wait_send()


def solution(mesh):
    S, T = mesh.shape["store"], mesh.shape["tensor"]
    X = S // 2

    def shards(tokens, ids, slot, wg, wu, wd, ag, bg, au, bu, ad, bd):
        n, depth = tokens.shape
        ff = wg.shape[1]
        cols = wd.shape[1]
        rank = ag.shape[1]
        flat = lambda v: v.reshape(-1, v.shape[2])
        ag, bg, au, bu, ad, bd = map(flat, (ag, bg, au, bu, ad, bd))
        lanes = ag.shape[0]
        nc = ff // CHUNKS
        on = cols // OUT_CHUNKS
        rows = T * PAD
        q = rows // S
        groups = lanes // rank
        packed = (rows // groups, lanes)
        vm = pltpu.VMEM
        dma = lambda *shape: pltpu.SemaphoreType.DMA(shape)
        pair = lambda *shape: [dma(*shape), dma(*shape)]
        scratch = [
            vm((CHUNKS, depth, nc), BF),
            vm((CHUNKS, depth, nc), BF),
            vm((CHUNKS, nc, cols), BF),
            vm(ag.shape, BF),
            vm(bg.shape, BF),
            vm(au.shape, BF),
            vm(bu.shape, BF),
            vm(ad.shape, BF),
            vm(bd.shape, BF),
            vm((T, PAD, depth), BF),
            vm((rows, lanes), F32),
            vm((rows, lanes), F32),
            vm((CHUNKS, S, q, 2 * nc), F32),
            vm((CHUNKS, X, q, 2 * nc), BF),
            vm((CHUNKS, X, q, 2 * nc), BF),
            vm((CHUNKS, X - 1, q, 2 * nc), BF),
            vm((CHUNKS, X - 1, q, 2 * nc), BF),
            vm((CHUNKS, S, q, nc), BF),
            vm((rows, lanes), F32),
            vm((OUT_CHUNKS, rows, on), F32),
            vm((OUT_CHUNKS, T, PAD, on), BF),
            vm((OUT_CHUNKS, T - 1, PAD, on), BF),
            vm((2,) + packed, F32),
            vm((S - 1, 2) + packed, F32),
            vm((2,) + packed, F32),
            vm((T - 1, 2) + packed, F32),
            vm(packed, F32),
            vm((S - 1,) + packed, F32),
            vm(packed, F32),
            vm((T - 1,) + packed, F32),
            dma(3, CHUNKS),
            dma(6),
            *pair(T - 1),
            *pair(S - 1),
            *pair(T - 1),
            *pair(S - 1),
            *pair(T - 1),
            *pair(CHUNKS),
            *pair(CHUNKS, X - 1),
            *pair(CHUNKS),
            *pair(CHUNKS, X - 1),
            *pair(CHUNKS, X - 1),
            *pair(OUT_CHUNKS, T - 1),
        ]
        smem = pl.BlockSpec(memory_space=pltpu.SMEM)
        vmem = pl.BlockSpec(memory_space=pltpu.VMEM)
        hbm = pl.BlockSpec(memory_space=pl.ANY)
        return pl.pallas_call(
            functools.partial(kernel, S, T, rank),
            out_shape=jax.ShapeDtypeStruct((n, cols), BF),
            in_specs=[vmem, smem, smem] + [hbm] * 9,
            out_specs=vmem,
            scratch_shapes=scratch,
            compiler_params=pltpu.CompilerParams(
                collective_id=0, has_side_effects=True, vmem_limit_bytes=60 * 1024 * 1024
            ),
        )(tokens, ids, slot, wg, wu, wd, ag, bg, au, bu, ad, bd)

    return jax.shard_map(
        shards,
        mesh=mesh,
        in_specs=(
            P(("groups", "tensor"), "store"),
            P("groups"),
            P(),
            P("store", "tensor"),
            P("store", "tensor"),
            P("tensor", "store"),
            P("tensor", None, "store"),
            P("store", None, "tensor"),
            P("tensor", None, "store"),
            P("store", None, "tensor"),
            P("store", None, "tensor"),
            P("tensor", None, "store"),
        ),
        out_specs=P(("groups", "tensor"), "store"),
        check_vma=False,
    )
```

```python
import functools

import jax
import jax.numpy as jnp
from jax import lax
from jax.experimental import pallas as pl
from jax.experimental.pallas import tpu as pltpu
from jax.sharding import PartitionSpec as P

MESH = pl.DeviceIdType.MESH
BF = jnp.bfloat16
F32 = jnp.float32
PAD = 16
CHUNKS = 7
OUT_CHUNKS = 4
SPLIT = 2
EARLY = 3
AHEAD = 5
HOLD = 2
WINDOW = 6
FIRST = 0
LAG_B, LAG_H, LAG_F, LAG_D = 1, 3, 5, 6


def plan():
    order = []
    for i in range(CHUNKS + LAG_D):
        steps = [("m", i)] if AHEAD <= i < CHUNKS else []
        steps += [("a", i), ("b", i - LAG_B), ("h", i - LAG_H), ("f", i - LAG_F), ("l", i - LAG_D)]
        if i - LAG_D < CHUNKS - HOLD:
            steps += [("d", i - LAG_D)]
        order += [(kind, j) for kind, j in steps if 0 <= j < CHUNKS]
    return order


ORDER = plan()


def nt_dot(a, b):
    return lax.dot_general(a, b, (((1,), (1,)), ((), ())), preferred_element_type=F32)


def kernel(
    S,
    T,
    rank,
    tok_ref,
    ids_ref,
    slot_ref,
    wg_hbm,
    wu_hbm,
    wd_hbm,
    ag_hbm,
    bg_hbm,
    au_hbm,
    bu_hbm,
    ad_hbm,
    bd_hbm,
    out_ref,
    wg,
    wu,
    wd,
    ag,
    bg,
    au,
    bu,
    ad,
    bd,
    tok,
    hot_t,
    hot_s,
    acc,
    send_a,
    recv_a,
    send_b,
    recv_b,
    hid,
    lacc,
    oacc,
    osend,
    orecv,
    low_mine,
    low_store,
    low_sum,
    low_tensor,
    dlow_mine,
    dlow_store,
    dlow_sum,
    dlow_tensor,
    w_sem,
    f_sem,
    tok_ss,
    tok_rs,
    ls_ss,
    ls_rs,
    lt_ss,
    lt_rs,
    ds_ss,
    ds_rs,
    dt_ss,
    dt_rs,
    a_ss,
    a_rs,
    b_ss,
    b_rs,
    h_ss,
    h_rs,
    g_ss,
    g_rs,
    k_ss,
    k_rs,
    o_ss,
    o_rs,
):
    X = S // 2
    s = lax.axis_index("store")
    t = lax.axis_index("tensor")
    x, c = s // 2, s % 2
    sib = x * 2 + (1 - c)
    n = tok_ref.shape[0]
    rows = T * PAD
    kd = tok.shape[3]
    nc = wg.shape[2]
    lanes = ag.shape[0]
    groups = lanes // rank
    on = oacc.shape[2]

    def weight(hbm, buf, j, sem):
        return pltpu.make_async_copy(hbm.at[:, pl.ds(j * nc, nc)], buf.at[j], sem)

    cg = [weight(wg_hbm, wg, j, w_sem.at[0, j]) for j in range(CHUNKS)]
    cu = [weight(wu_hbm, wu, j, w_sem.at[1, j]) for j in range(CHUNKS)]
    cd = [
        pltpu.make_async_copy(wd_hbm.at[pl.ds(j * nc, nc), :], wd.at[j], w_sem.at[2, j])
        for j in range(CHUNKS)
    ]
    cag = pltpu.make_async_copy(ag_hbm, ag, f_sem.at[0])
    cau = pltpu.make_async_copy(au_hbm, au, f_sem.at[1])
    cbg = pltpu.make_async_copy(bg_hbm, bg, f_sem.at[2])
    cbu = pltpu.make_async_copy(bu_hbm, bu, f_sem.at[3])
    cad = pltpu.make_async_copy(ad_hbm, ad, f_sem.at[4])
    cbd = pltpu.make_async_copy(bd_hbm, bd, f_sem.at[5])

    barrier = pltpu.get_barrier_semaphore()
    for d in range(1, S):
        pl.semaphore_signal(
            barrier, inc=1, device_id={"store": (s + d) % S}, device_id_type=MESH
        )
    for d in range(1, T):
        pl.semaphore_signal(
            barrier, inc=1, device_id={"tensor": (t + d) % T}, device_id_type=MESH
        )
    line = [cag, cau]
    for j in range(CHUNKS):
        line += [cg[j], cu[j]]
        if j == 1:
            line += [cbg, cbu]
    line += [cad] + cd + [cbd]
    waited = []
    for copy in line[:WINDOW]:
        copy.start()

    def need(copy):
        while not any(copy is w for w in waited):
            k = len(waited)
            line[k].wait()
            waited.append(line[k])
            if k + WINDOW < len(line):
                line[k + WINDOW].start()

    for h in range(SPLIT):
        tok[h, t] = jnp.zeros((PAD, kd), BF)
        tok[h, t, 0:n, :] = tok_ref[:, h * kd : (h + 1) * kd]
    pl.semaphore_wait(barrier, S + T - 2)

    def remote(src, dst, ss, rs, axis, index):
        return pltpu.make_async_remote_copy(
            src_ref=src,
            dst_ref=dst,
            send_sem=ss,
            recv_sem=rs,
            device_id={axis: index},
            device_id_type=MESH,
        )

    sent = []

    def go(copy):
        copy.start()
        sent.append(copy)
        return copy

    tcopies = [
        [
            go(
                remote(
                    tok.at[h, t],
                    tok.at[h, t],
                    tok_ss.at[h, d - 1],
                    tok_rs.at[h, d - 1],
                    "tensor",
                    (t + d) % T,
                )
            )
            for d in range(1, T)
        ]
        for h in range(SPLIT)
    ]

    lane_group = lax.broadcasted_iota(jnp.int32, (1, lanes), 1) // rank
    hot_t[...] = jnp.zeros_like(hot_t)
    hot_s[...] = jnp.zeros_like(hot_s)

    def mark(r, carry):
        place = slot_ref[ids_ref[r]]
        row = (r // n) * PAD + r % n
        hot_t[pl.ds(row, 1), :] = jnp.where(lane_group == place - t * groups, 1.0, 0.0)
        hot_s[pl.ds(row, 1), :] = jnp.where(lane_group == place - s * groups, 1.0, 0.0)
        return carry

    lax.fori_loop(0, n * T, mark, 0)

    fold = (
        lax.broadcasted_iota(jnp.int32, (lanes, lanes), 0) % rank
        == lax.broadcasted_iota(jnp.int32, (lanes, lanes), 1) % rank
    )
    own_group = (
        lax.broadcasted_iota(jnp.int32, (rows, lanes), 0) % groups
        == lax.broadcasted_iota(jnp.int32, (rows, lanes), 1) // rank
    )

    def pack(part):
        spread = jnp.dot(
            part, fold.astype(F32), precision=lax.Precision.HIGHEST, preferred_element_type=F32
        )
        spread = jnp.where(own_group, spread, 0.0)
        return jnp.sum(spread.reshape(rows // groups, groups, lanes), axis=1)

    def unpack(packed, hot):
        spread = jnp.broadcast_to(packed[:, None, :], (rows // groups, groups, lanes))
        spread = jnp.where(own_group, spread.reshape(rows, lanes), 0.0).astype(BF)
        low = jnp.dot(spread, fold.astype(F32).astype(BF), preferred_element_type=F32)
        return (low * hot[...]).astype(BF)

    def exchange(mine, slots, ss, rs, axis, me, size):
        return [
            go(remote(mine, slots.at[d - 1], ss.at[d - 1], rs.at[d - 1], axis, (me + d) % size))
            for d in range(1, size)
        ]

    def gather_sum(mine, slots, copies):
        total = mine[...]
        for d, copy in enumerate(copies):
            copy.wait_recv()
            total = total + slots[d]
        return total

    q = rows // S

    def half(h):
        return tok[h].reshape(rows, kd)

    def main_part(j, h):
        ks = slice(h * kd, (h + 1) * kd)
        for first, buf, copies in ((0, wg, cg), (nc, wu, cu)):
            need(copies[j])
            v = jnp.dot(half(h), buf[j, ks, :], preferred_element_type=F32).reshape(S, q, nc)
            if h > 0:
                v = v + acc[j, :, :, first : first + nc]
            acc[j, :, :, first : first + nc] = v

    def main(j):
        need(cu[j])
        for first, buf in ((0, wg), (nc, wu)):
            v = 0.0
            for h in range(SPLIT):
                v = v + jnp.dot(
                    half(h), buf[j, h * kd : (h + 1) * kd, :], preferred_element_type=F32
                )
            acc[j, :, :, first : first + nc] = v.reshape(S, q, nc)

    lows = [0.0, 0.0]
    for h in range(SPLIT):
        need(cu[h + FIRST])
        for copy in tcopies[h]:
            copy.wait_recv()
        for k, buf in enumerate((ag, au)):
            lows[k] = lows[k] + nt_dot(half(h), buf[:, h * kd : (h + 1) * kd])
        if h < SPLIT - 1:
            for j in range(EARLY):
                main_part(j, h)
    low_mine[0] = pack(lows[0] * hot_t[...])
    low_mine[1] = pack(lows[1] * hot_t[...])
    ls = exchange(low_mine, low_store, ls_ss, ls_rs, "store", s, S)

    acopies, bcopies, hcopies, gcopies, kcopies = {}, {}, {}, {}, {}

    def finish(j, spread_g, spread_u):
        cols = pl.ds(j * nc, nc)
        acc[j, :, :, 0:nc] += jnp.dot(
            spread_g, bg[:, cols], preferred_element_type=F32
        ).reshape(S, q, nc)
        acc[j, :, :, nc:] += jnp.dot(
            spread_u, bu[:, cols], preferred_element_type=F32
        ).reshape(S, q, nc)
        for k in range(X):
            send_a[j, k] = acc[j, 2 * k + (1 - c)].astype(BF)
        acopies[j] = go(remote(send_a.at[j], recv_a.at[j], a_ss.at[j], a_rs.at[j], "store", sib))

    def stage_b(j):
        acopies[j].wait_recv()
        bcopies[j] = []
        for d in range(1, X):
            xo = (x + d) % X
            send_b[j, d - 1] = (acc[j, 2 * xo + c] + recv_a[j, xo].astype(F32)).astype(BF)
            bcopies[j].append(
                go(
                    remote(
                        send_b.at[j, d - 1],
                        recv_b.at[j, d - 1],
                        b_ss.at[j, d - 1],
                        b_rs.at[j, d - 1],
                        "store",
                        xo * 2 + c,
                    )
                )
            )

    def stage_h(j):
        total = acc[j, s] + recv_a[j, x].astype(F32)
        for d in range(1, X):
            bcopies[j][d - 1].wait_recv()
            total = total + recv_b[j, d - 1].astype(F32)
        gate, up = total[:, 0:nc], total[:, nc:]
        hid[j, s] = (gate / (1.0 + jnp.exp(-gate)) * up).astype(BF)
        gcopies[j] = [
            go(
                remote(
                    hid.at[j, s],
                    hid.at[j, s],
                    g_ss.at[j, d - 1],
                    g_rs.at[j, d - 1],
                    "store",
                    ((x + d) % X) * 2 + c,
                )
            )
            for d in range(1, X)
        ]
        hcopies[j] = go(
            remote(hid.at[j, s], hid.at[j, s], h_ss.at[j], h_rs.at[j], "store", sib)
        )

    def stage_f(j):
        kcopies[j] = []
        for d in range(1, X):
            gcopies[j][d - 1].wait_recv()
            origin = ((x - d + X) % X) * 2 + c
            kcopies[j].append(
                go(
                    remote(
                        hid.at[j, origin],
                        hid.at[j, origin],
                        k_ss.at[j, d - 1],
                        k_rs.at[j, d - 1],
                        "store",
                        sib,
                    )
                )
            )

    def stage_l(j):
        hcopies[j].wait_recv()
        for copy in kcopies[j]:
            copy.wait_recv()
        if j == 0:
            need(cad)
        low = nt_dot(hid[j].reshape(rows, nc), ad[:, pl.ds(j * nc, nc)])
        lacc[...] = low if j == 0 else lacc[...] + low
        if j == CHUNKS - 1:
            dlow_mine[...] = pack(lacc[...] * hot_s[...])
            return exchange(dlow_mine, dlow_store, ds_ss, ds_rs, "store", s, S)

    def stage_d(j):
        need(cd[j])
        for k in range(OUT_CHUNKS):
            o = jnp.dot(
                hid[j].reshape(rows, nc), wd[j, :, k * on : (k + 1) * on], preferred_element_type=F32
            )
            oacc[k] = o if j == 0 else oacc[k] + o

    for j in range(EARLY):
        main_part(j, SPLIT - 1)
    low_sum[...] = gather_sum(low_mine, low_store, ls)
    lt = exchange(low_sum, low_tensor, lt_ss, lt_rs, "tensor", t, T)
    for j in range(EARLY, AHEAD):
        main(j)
    low = gather_sum(low_sum, low_tensor, lt)
    spread_g = unpack(low[0], hot_s)
    spread_u = unpack(low[1], hot_s)
    need(cbu)

    copies = None
    for kind, j in ORDER:
        if kind == "m":
            main(j)
        elif kind == "a":
            finish(j, spread_g, spread_u)
        elif kind == "b":
            stage_b(j)
        elif kind == "h":
            stage_h(j)
        elif kind == "f":
            stage_f(j)
        elif kind == "l":
            copies = stage_l(j) or copies
        elif kind == "d":
            stage_d(j)

    dlow_sum[...] = gather_sum(dlow_mine, dlow_store, copies)
    copies = exchange(dlow_sum, dlow_tensor, dt_ss, dt_rs, "tensor", t, T)
    for j in range(CHUNKS - HOLD, CHUNKS):
        stage_d(j)
    dlow = gather_sum(dlow_sum, dlow_tensor, copies)
    spread_d = unpack(dlow, hot_t)
    need(cbd)
    ocopies = []
    own = []
    for k in range(OUT_CHUNKS):
        o = oacc[k] + jnp.dot(
            spread_d, bd[:, k * on : (k + 1) * on], preferred_element_type=F32
        )
        oacc[k] = o
        osend[k] = o.reshape(T, PAD, on).astype(BF)
        ocopies.append(
            [
                go(
                    remote(
                        osend.at[k, (t + d) % T],
                        orecv.at[k, d - 1],
                        o_ss.at[k, d - 1],
                        o_rs.at[k, d - 1],
                        "tensor",
                        (t + d) % T,
                    )
                )
                for d in range(1, T)
            ]
        )
    for k in range(OUT_CHUNKS):
        total = oacc[k, pl.ds(pl.multiple_of(t * PAD, PAD), PAD), :]
        for d in range(1, T):
            ocopies[k][d - 1].wait_recv()
            total = total + orecv[k, d - 1].astype(F32)
        out_ref[:, k * on : (k + 1) * on] = total[0:n].astype(BF)
    for copy in sent:
        copy.wait_send()


def solution(mesh):
    S, T = mesh.shape["store"], mesh.shape["tensor"]
    X = S // 2

    def shards(tokens, ids, slot, wg, wu, wd, ag, bg, au, bu, ad, bd):
        n, depth = tokens.shape
        ff = wg.shape[1]
        cols = wd.shape[1]
        rank = ag.shape[1]
        flat = lambda v: v.reshape(-1, v.shape[2])
        ag, bg, au, bu, ad, bd = map(flat, (ag, bg, au, bu, ad, bd))
        lanes = ag.shape[0]
        nc = ff // CHUNKS
        on = cols // OUT_CHUNKS
        rows = T * PAD
        q = rows // S
        groups = lanes // rank
        packed = (rows // groups, lanes)
        vm = pltpu.VMEM
        dma = lambda *shape: pltpu.SemaphoreType.DMA(shape)
        pair = lambda *shape: [dma(*shape), dma(*shape)]
        scratch = [
            vm((CHUNKS, depth, nc), BF),
            vm((CHUNKS, depth, nc), BF),
            vm((CHUNKS, nc, cols), BF),
            vm(ag.shape, BF),
            vm(bg.shape, BF),
            vm(au.shape, BF),
            vm(bu.shape, BF),
            vm(ad.shape, BF),
            vm(bd.shape, BF),
            vm((SPLIT, T, PAD, depth // SPLIT), BF),
            vm((rows, lanes), F32),
            vm((rows, lanes), F32),
            vm((CHUNKS, S, q, 2 * nc), F32),
            vm((CHUNKS, X, q, 2 * nc), BF),
            vm((CHUNKS, X, q, 2 * nc), BF),
            vm((CHUNKS, X - 1, q, 2 * nc), BF),
            vm((CHUNKS, X - 1, q, 2 * nc), BF),
            vm((CHUNKS, S, q, nc), BF),
            vm((rows, lanes), F32),
            vm((OUT_CHUNKS, rows, on), F32),
            vm((OUT_CHUNKS, T, PAD, on), BF),
            vm((OUT_CHUNKS, T - 1, PAD, on), BF),
            vm((2,) + packed, F32),
            vm((S - 1, 2) + packed, F32),
            vm((2,) + packed, F32),
            vm((T - 1, 2) + packed, F32),
            vm(packed, F32),
            vm((S - 1,) + packed, F32),
            vm(packed, F32),
            vm((T - 1,) + packed, F32),
            dma(3, CHUNKS),
            dma(6),
            *pair(SPLIT, T - 1),
            *pair(S - 1),
            *pair(T - 1),
            *pair(S - 1),
            *pair(T - 1),
            *pair(CHUNKS),
            *pair(CHUNKS, X - 1),
            *pair(CHUNKS),
            *pair(CHUNKS, X - 1),
            *pair(CHUNKS, X - 1),
            *pair(OUT_CHUNKS, T - 1),
        ]
        smem = pl.BlockSpec(memory_space=pltpu.SMEM)
        vmem = pl.BlockSpec(memory_space=pltpu.VMEM)
        hbm = pl.BlockSpec(memory_space=pl.ANY)
        return pl.pallas_call(
            functools.partial(kernel, S, T, rank),
            out_shape=jax.ShapeDtypeStruct((n, cols), BF),
            in_specs=[vmem, smem, smem] + [hbm] * 9,
            out_specs=vmem,
            scratch_shapes=scratch,
            compiler_params=pltpu.CompilerParams(
                collective_id=0, has_side_effects=True, vmem_limit_bytes=60 * 1024 * 1024
            ),
        )(tokens, ids, slot, wg, wu, wd, ag, bg, au, bu, ad, bd)

    return jax.shard_map(
        shards,
        mesh=mesh,
        in_specs=(
            P(("groups", "tensor"), "store"),
            P("groups"),
            P(),
            P("store", "tensor"),
            P("store", "tensor"),
            P("tensor", "store"),
            P("tensor", None, "store"),
            P("store", None, "tensor"),
            P("tensor", None, "store"),
            P("store", None, "tensor"),
            P("store", None, "tensor"),
            P("tensor", None, "store"),
        ),
        out_specs=P(("groups", "tensor"), "store"),
        check_vma=False,
    )
```

```python
import functools

import jax
import jax.numpy as jnp
from jax import lax
from jax.experimental import pallas as pl
from jax.experimental.pallas import tpu as pltpu
from jax.sharding import PartitionSpec as P

MESH = pl.DeviceIdType.MESH
BF = jnp.bfloat16
F32 = jnp.float32
PAD = 16
CHUNKS = 7
OUT_CHUNKS = 4
SPLIT = 2
EARLY = 1
MID = 2
AHEAD = 4
HOLD = 2
WINDOW = 6
FIRST = 0
LAG_B, LAG_H, LAG_D = 1, 3, 5


def plan():
    order = []
    for i in range(CHUNKS + LAG_D):
        steps = [("m", i)] if AHEAD <= i < CHUNKS else []
        steps += [("a", i), ("b", i - LAG_B), ("h", i - LAG_H), ("l", i - LAG_D)]
        if i - LAG_D < CHUNKS - HOLD:
            steps += [("d", i - LAG_D)]
        order += [(kind, j) for kind, j in steps if 0 <= j < CHUNKS]
    return order


ORDER = plan()


def nt_dot(a, b):
    return lax.dot_general(a, b, (((1,), (1,)), ((), ())), preferred_element_type=F32)


def kernel(
    S,
    T,
    rank,
    tok_ref,
    ids_ref,
    slot_ref,
    wg_hbm,
    wu_hbm,
    wd_hbm,
    ag_hbm,
    bg_hbm,
    au_hbm,
    bu_hbm,
    ad_hbm,
    bd_hbm,
    out_ref,
    wg,
    wu,
    wd,
    ag,
    bg,
    au,
    bu,
    ad,
    bd,
    tok,
    hot_t,
    hot_s,
    acc,
    send_a,
    recv_a,
    send_b,
    recv_b,
    hid,
    lacc,
    oacc,
    osend,
    orecv,
    low_mine,
    low_store,
    low_sum,
    low_tensor,
    dlow_mine,
    dlow_store,
    dlow_sum,
    dlow_tensor,
    w_sem,
    f_sem,
    tok_ss,
    tok_rs,
    ls_ss,
    ls_rs,
    lt_ss,
    lt_rs,
    ds_ss,
    ds_rs,
    dt_ss,
    dt_rs,
    a_ss,
    a_rs,
    b_ss,
    b_rs,
    h_ss,
    h_rs,
    g_ss,
    g_rs,
    k_ss,
    k_rs,
    o_ss,
    o_rs,
):
    X = S // 2
    s = lax.axis_index("store")
    t = lax.axis_index("tensor")
    x, c = s // 2, s % 2
    sib = x * 2 + (1 - c)
    n = tok_ref.shape[0]
    rows = T * PAD
    kd = tok.shape[3]
    nc = wg.shape[2]
    lanes = ag.shape[0]
    groups = lanes // rank
    on = oacc.shape[2]

    def weight(hbm, buf, j, sem):
        return pltpu.make_async_copy(hbm.at[:, pl.ds(j * nc, nc)], buf.at[j], sem)

    cg = [weight(wg_hbm, wg, j, w_sem.at[0, j]) for j in range(CHUNKS)]
    cu = [weight(wu_hbm, wu, j, w_sem.at[1, j]) for j in range(CHUNKS)]
    cd = [
        pltpu.make_async_copy(wd_hbm.at[pl.ds(j * nc, nc), :], wd.at[j], w_sem.at[2, j])
        for j in range(CHUNKS)
    ]
    cag = pltpu.make_async_copy(ag_hbm, ag, f_sem.at[0])
    cau = pltpu.make_async_copy(au_hbm, au, f_sem.at[1])
    cbg = pltpu.make_async_copy(bg_hbm, bg, f_sem.at[2])
    cbu = pltpu.make_async_copy(bu_hbm, bu, f_sem.at[3])
    cad = pltpu.make_async_copy(ad_hbm, ad, f_sem.at[4])
    cbd = pltpu.make_async_copy(bd_hbm, bd, f_sem.at[5])

    barrier = pltpu.get_barrier_semaphore()
    for d in range(1, S):
        pl.semaphore_signal(
            barrier, inc=1, device_id={"store": (s + d) % S}, device_id_type=MESH
        )
    for d in range(1, T):
        pl.semaphore_signal(
            barrier, inc=1, device_id={"tensor": (t + d) % T}, device_id_type=MESH
        )
    line = [cag, cau]
    for j in range(CHUNKS):
        line += [cg[j], cu[j]]
        if j == 1:
            line += [cbg, cbu]
    line += [cad] + cd + [cbd]
    waited = []
    for copy in line[:WINDOW]:
        copy.start()

    def need(copy):
        while not any(copy is w for w in waited):
            k = len(waited)
            line[k].wait()
            waited.append(line[k])
            if k + WINDOW < len(line):
                line[k + WINDOW].start()

    for h in range(SPLIT):
        tok[h, t] = jnp.zeros((PAD, kd), BF)
        tok[h, t, 0:n, :] = tok_ref[:, h * kd : (h + 1) * kd]
    pl.semaphore_wait(barrier, S + T - 2)

    def remote(src, dst, ss, rs, axis, index):
        return pltpu.make_async_remote_copy(
            src_ref=src,
            dst_ref=dst,
            send_sem=ss,
            recv_sem=rs,
            device_id={axis: index},
            device_id_type=MESH,
        )

    sent = []

    def go(copy):
        copy.start()
        sent.append(copy)
        return copy

    tcopies = [
        [
            go(
                remote(
                    tok.at[h, t],
                    tok.at[h, t],
                    tok_ss.at[h, d - 1],
                    tok_rs.at[h, d - 1],
                    "tensor",
                    (t + d) % T,
                )
            )
            for d in range(1, T)
        ]
        for h in range(SPLIT)
    ]

    lane_group = lax.broadcasted_iota(jnp.int32, (1, lanes), 1) // rank
    hot_t[...] = jnp.zeros_like(hot_t)
    hot_s[...] = jnp.zeros_like(hot_s)

    def mark(r, carry):
        place = slot_ref[ids_ref[r]]
        row = (r // n) * PAD + r % n
        hot_t[pl.ds(row, 1), :] = jnp.where(lane_group == place - t * groups, 1.0, 0.0)
        hot_s[pl.ds(row, 1), :] = jnp.where(lane_group == place - s * groups, 1.0, 0.0)
        return carry

    lax.fori_loop(0, n * T, mark, 0)

    fold = (
        lax.broadcasted_iota(jnp.int32, (lanes, lanes), 0) % rank
        == lax.broadcasted_iota(jnp.int32, (lanes, lanes), 1) % rank
    )
    own_group = (
        lax.broadcasted_iota(jnp.int32, (rows, lanes), 0) % groups
        == lax.broadcasted_iota(jnp.int32, (rows, lanes), 1) // rank
    )

    def pack(part):
        spread = jnp.dot(
            part, fold.astype(F32), precision=lax.Precision.HIGHEST, preferred_element_type=F32
        )
        spread = jnp.where(own_group, spread, 0.0)
        return jnp.sum(spread.reshape(rows // groups, groups, lanes), axis=1)

    def unpack(packed, hot):
        spread = jnp.broadcast_to(packed[:, None, :], (rows // groups, groups, lanes))
        spread = jnp.where(own_group, spread.reshape(rows, lanes), 0.0).astype(BF)
        low = jnp.dot(spread, fold.astype(F32).astype(BF), preferred_element_type=F32)
        return (low * hot[...]).astype(BF)

    def exchange(mine, slots, ss, rs, axis, me, size):
        return [
            go(remote(mine, slots.at[d - 1], ss.at[d - 1], rs.at[d - 1], axis, (me + d) % size))
            for d in range(1, size)
        ]

    def gather_sum(mine, slots, copies):
        total = mine[...]
        for d, copy in enumerate(copies):
            copy.wait_recv()
            total = total + slots[d]
        return total

    q = rows // S

    def half(h):
        return tok[h].reshape(rows, kd)

    def main_part(j, h):
        ks = slice(h * kd, (h + 1) * kd)
        for first, buf, copies in ((0, wg, cg), (nc, wu, cu)):
            need(copies[j])
            v = jnp.dot(half(h), buf[j, ks, :], preferred_element_type=F32).reshape(S, q, nc)
            if h > 0:
                v = v + acc[j, :, :, first : first + nc]
            acc[j, :, :, first : first + nc] = v

    def main(j):
        need(cu[j])
        for first, buf in ((0, wg), (nc, wu)):
            v = 0.0
            for h in range(SPLIT):
                v = v + jnp.dot(
                    half(h), buf[j, h * kd : (h + 1) * kd, :], preferred_element_type=F32
                )
            acc[j, :, :, first : first + nc] = v.reshape(S, q, nc)

    lows = [0.0, 0.0]
    for h in range(SPLIT):
        need(cu[h + FIRST])
        for copy in tcopies[h]:
            copy.wait_recv()
        for k, buf in enumerate((ag, au)):
            lows[k] = lows[k] + nt_dot(half(h), buf[:, h * kd : (h + 1) * kd])
        if h < SPLIT - 1:
            for j in range(EARLY):
                main_part(j, h)
    low_mine[0] = pack(lows[0] * hot_t[...])
    low_mine[1] = pack(lows[1] * hot_t[...])
    ls = exchange(low_mine, low_store, ls_ss, ls_rs, "store", s, S)

    acopies, bcopies, hcopies, gcopies, kcopies = {}, {}, {}, {}, {}

    def finish(j, spread_g, spread_u):
        cols = pl.ds(j * nc, nc)
        acc[j, :, :, 0:nc] += jnp.dot(
            spread_g, bg[:, cols], preferred_element_type=F32
        ).reshape(S, q, nc)
        acc[j, :, :, nc:] += jnp.dot(
            spread_u, bu[:, cols], preferred_element_type=F32
        ).reshape(S, q, nc)
        for k in range(X):
            send_a[j, k] = acc[j, 2 * k + (1 - c)].astype(BF)
        acopies[j] = go(remote(send_a.at[j], recv_a.at[j], a_ss.at[j], a_rs.at[j], "store", sib))

    def stage_b(j):
        acopies[j].wait_recv()
        bcopies[j] = []
        for d in range(1, X):
            xo = (x + d) % X
            send_b[j, d - 1] = (acc[j, 2 * xo + c] + recv_a[j, xo].astype(F32)).astype(BF)
            bcopies[j].append(
                go(
                    remote(
                        send_b.at[j, d - 1],
                        recv_b.at[j, d - 1],
                        b_ss.at[j, d - 1],
                        b_rs.at[j, d - 1],
                        "store",
                        xo * 2 + c,
                    )
                )
            )

    def stage_h(j):
        total = acc[j, s] + recv_a[j, x].astype(F32)
        for d in range(1, X):
            bcopies[j][d - 1].wait_recv()
            total = total + recv_b[j, d - 1].astype(F32)
        gate, up = total[:, 0:nc], total[:, nc:]
        hid[j, s] = (gate / (1.0 + jnp.exp(-gate)) * up).astype(BF)
        def peers(ss, rs, core):
            return [
                go(
                    remote(
                        hid.at[j, s],
                        hid.at[j, s],
                        ss.at[j, d - 1],
                        rs.at[j, d - 1],
                        "store",
                        ((x + d) % X) * 2 + core,
                    )
                )
                for d in range(1, X)
            ]

        gcopies[j] = peers(g_ss, g_rs, c)
        kcopies[j] = peers(k_ss, k_rs, 1 - c)
        hcopies[j] = go(
            remote(hid.at[j, s], hid.at[j, s], h_ss.at[j], h_rs.at[j], "store", sib)
        )

    def stage_l(j):
        hcopies[j].wait_recv()
        for copy in gcopies[j] + kcopies[j]:
            copy.wait_recv()
        if j == 0:
            need(cad)
        low = nt_dot(hid[j].reshape(rows, nc), ad[:, pl.ds(j * nc, nc)])
        lacc[...] = low if j == 0 else lacc[...] + low
        if j == CHUNKS - 1:
            dlow_mine[...] = pack(lacc[...] * hot_s[...])
            return exchange(dlow_mine, dlow_store, ds_ss, ds_rs, "store", s, S)

    def stage_d(j):
        need(cd[j])
        for k in range(OUT_CHUNKS):
            o = jnp.dot(
                hid[j].reshape(rows, nc), wd[j, :, k * on : (k + 1) * on], preferred_element_type=F32
            )
            oacc[k] = o if j == 0 else oacc[k] + o

    for j in range(EARLY):
        main_part(j, SPLIT - 1)
    for j in range(EARLY, MID):
        main(j)
    low_sum[...] = gather_sum(low_mine, low_store, ls)
    lt = exchange(low_sum, low_tensor, lt_ss, lt_rs, "tensor", t, T)
    for j in range(MID, AHEAD):
        main(j)
    low = gather_sum(low_sum, low_tensor, lt)
    spread_g = unpack(low[0], hot_s)
    spread_u = unpack(low[1], hot_s)
    need(cbu)

    copies = None
    for kind, j in ORDER:
        if kind == "m":
            main(j)
        elif kind == "a":
            finish(j, spread_g, spread_u)
        elif kind == "b":
            stage_b(j)
        elif kind == "h":
            stage_h(j)
        elif kind == "l":
            copies = stage_l(j) or copies
        elif kind == "d":
            stage_d(j)

    dlow_sum[...] = gather_sum(dlow_mine, dlow_store, copies)
    copies = exchange(dlow_sum, dlow_tensor, dt_ss, dt_rs, "tensor", t, T)
    for j in range(CHUNKS - HOLD, CHUNKS):
        stage_d(j)
    dlow = gather_sum(dlow_sum, dlow_tensor, copies)
    spread_d = unpack(dlow, hot_t)
    need(cbd)
    ocopies = []
    own = []
    for k in range(OUT_CHUNKS):
        o = oacc[k] + jnp.dot(
            spread_d, bd[:, k * on : (k + 1) * on], preferred_element_type=F32
        )
        oacc[k] = o
        osend[k] = o.reshape(T, PAD, on).astype(BF)
        ocopies.append(
            [
                go(
                    remote(
                        osend.at[k, (t + d) % T],
                        orecv.at[k, d - 1],
                        o_ss.at[k, d - 1],
                        o_rs.at[k, d - 1],
                        "tensor",
                        (t + d) % T,
                    )
                )
                for d in range(1, T)
            ]
        )
    for k in range(OUT_CHUNKS):
        total = oacc[k, pl.ds(pl.multiple_of(t * PAD, PAD), PAD), :]
        for d in range(1, T):
            ocopies[k][d - 1].wait_recv()
            total = total + orecv[k, d - 1].astype(F32)
        out_ref[:, k * on : (k + 1) * on] = total[0:n].astype(BF)
    for copy in sent:
        copy.wait_send()


def solution(mesh):
    S, T = mesh.shape["store"], mesh.shape["tensor"]
    X = S // 2

    def shards(tokens, ids, slot, wg, wu, wd, ag, bg, au, bu, ad, bd):
        n, depth = tokens.shape
        ff = wg.shape[1]
        cols = wd.shape[1]
        rank = ag.shape[1]
        flat = lambda v: v.reshape(-1, v.shape[2])
        ag, bg, au, bu, ad, bd = map(flat, (ag, bg, au, bu, ad, bd))
        lanes = ag.shape[0]
        nc = ff // CHUNKS
        on = cols // OUT_CHUNKS
        rows = T * PAD
        q = rows // S
        groups = lanes // rank
        packed = (rows // groups, lanes)
        vm = pltpu.VMEM
        dma = lambda *shape: pltpu.SemaphoreType.DMA(shape)
        pair = lambda *shape: [dma(*shape), dma(*shape)]
        scratch = [
            vm((CHUNKS, depth, nc), BF),
            vm((CHUNKS, depth, nc), BF),
            vm((CHUNKS, nc, cols), BF),
            vm(ag.shape, BF),
            vm(bg.shape, BF),
            vm(au.shape, BF),
            vm(bu.shape, BF),
            vm(ad.shape, BF),
            vm(bd.shape, BF),
            vm((SPLIT, T, PAD, depth // SPLIT), BF),
            vm((rows, lanes), F32),
            vm((rows, lanes), F32),
            vm((CHUNKS, S, q, 2 * nc), F32),
            vm((CHUNKS, X, q, 2 * nc), BF),
            vm((CHUNKS, X, q, 2 * nc), BF),
            vm((CHUNKS, X - 1, q, 2 * nc), BF),
            vm((CHUNKS, X - 1, q, 2 * nc), BF),
            vm((CHUNKS, S, q, nc), BF),
            vm((rows, lanes), F32),
            vm((OUT_CHUNKS, rows, on), F32),
            vm((OUT_CHUNKS, T, PAD, on), BF),
            vm((OUT_CHUNKS, T - 1, PAD, on), BF),
            vm((2,) + packed, F32),
            vm((S - 1, 2) + packed, F32),
            vm((2,) + packed, F32),
            vm((T - 1, 2) + packed, F32),
            vm(packed, F32),
            vm((S - 1,) + packed, F32),
            vm(packed, F32),
            vm((T - 1,) + packed, F32),
            dma(3, CHUNKS),
            dma(6),
            *pair(SPLIT, T - 1),
            *pair(S - 1),
            *pair(T - 1),
            *pair(S - 1),
            *pair(T - 1),
            *pair(CHUNKS),
            *pair(CHUNKS, X - 1),
            *pair(CHUNKS),
            *pair(CHUNKS, X - 1),
            *pair(CHUNKS, X - 1),
            *pair(OUT_CHUNKS, T - 1),
        ]
        smem = pl.BlockSpec(memory_space=pltpu.SMEM)
        vmem = pl.BlockSpec(memory_space=pltpu.VMEM)
        hbm = pl.BlockSpec(memory_space=pl.ANY)
        return pl.pallas_call(
            functools.partial(kernel, S, T, rank),
            out_shape=jax.ShapeDtypeStruct((n, cols), BF),
            in_specs=[vmem, smem, smem] + [hbm] * 9,
            out_specs=vmem,
            scratch_shapes=scratch,
            compiler_params=pltpu.CompilerParams(
                collective_id=0, has_side_effects=True, vmem_limit_bytes=60 * 1024 * 1024
            ),
        )(tokens, ids, slot, wg, wu, wd, ag, bg, au, bu, ad, bd)

    return jax.shard_map(
        shards,
        mesh=mesh,
        in_specs=(
            P(("groups", "tensor"), "store"),
            P("groups"),
            P(),
            P("store", "tensor"),
            P("store", "tensor"),
            P("tensor", "store"),
            P("tensor", None, "store"),
            P("store", None, "tensor"),
            P("tensor", None, "store"),
            P("store", None, "tensor"),
            P("store", None, "tensor"),
            P("tensor", None, "store"),
        ),
        out_specs=P(("groups", "tensor"), "store"),
        check_vma=False,
    )
```
